512 devices in a mesh: replica: 32 (over x, z), expert: 16 (over y, core).
Axes of the slice: x: 4, y: 8, z: 8, core: 2. Of those that a mesh axis runs over, the one named last changes fastest.
Arguments:
- weights: bfloat16 [32, 3, 3072, 2048], P('replica', None, 'expert'), may hold values from -0.125 to 0.125
- tokens: bfloat16 [32, 2048, 2048], P('replica', 'expert'), may hold values from -6 to 6
- cotangent: bfloat16 [32, 2048, 2048], P('replica', 'expert'), may hold values from -6 to 6
- routes: int32 [32, 2048, 1], P('replica', 'expert'), may hold values from 0 to 3; in each aligned block of 128 rows (0 to 127, 128 to 255, ..., all dimensions but the last counted through in order) at most 44 rows name the same one
- gate_weights: float32 [32, 2048, 1], P('replica', 'expert'), may hold values from 0.25 to 1
- next_tokens: bfloat16 [32, 2048, 2048], P('replica', 'expert'), may hold values from -6 to 6
- next_routes: int32 [32, 2048, 1], P('replica', 'expert'), may hold values from 0 to 3; in each aligned block of 128 rows (0 to 127, 128 to 255, ..., all dimensions but the last counted through in order) at most 44 rows name the same one
- next_gates: float32 [32, 2048, 1], P('replica', 'expert'), may hold values from 0.25 to 1
- step_index: int32 [1], replicated, may hold values from 0 to 63
Outputs:
- token_codes: bfloat16 [32, 2048, 2048], P('replica', 'expert')
- token_scales: float32 [32, 2048], P('replica', 'expert')
The draws below stay inside these ranges and needn't reach their ends.
Inputs may be any that keep to these rules, and one draw needn't show every extreme that they name: `routes`: in the 128 tokens of one device, no expert is named more than 44 times, a bound that some block reaches; a token names 1 different experts. `next_routes`: in the 128 tokens of one device, no expert is named more than 44 times, a bound that some block reaches; a token names 1 different experts.
All inputs are finite; a program needn't handle non-finite values. Where the reference program divides by a largest or mean magnitude, that divisor is 1e-20 or more.
Results may differ from the reference program's by a relative error of at most 0.025.
Values may be sent and summed in bfloat16 or wider, within the bound.
A program may use at most 128 MiB of HBM per device.

```python
import math
import jax
import jax.numpy as jnp
import numpy as np
from jax import lax

D = 2048
FF = 768
EXPERTS = 4
TOP = 1
TOK_DEV = 128
CAP = 44
REPLICAS = 32
TOKENS = 2048
N_REPLICA = 32
N_EXPERT = 16


def level_of(key, dims, cuts, low, top_value):
    factor_of = 1.0
    for dim, parts in cuts:
        heights = jax.random.uniform(jax.random.fold_in(jax.random.fold_in(key, 6), dim), (parts,), jnp.float32, low / len(cuts), top_value / len(cuts))
        factor_of = factor_of * jnp.repeat(jnp.exp(heights), dims[dim] // parts).reshape((-1,) + (1,) * (len(dims) - 1 - dim))
    return factor_of


def shared_out(stream_key, own, number, rows, count, top, reach, lean):
    ranking = jax.random.permutation(stream_key, count)
    heavy_load, common = shares(count, rows * top, reach, lean, True), shares(count, rows * top, reach, lean, False)
    places = jnp.arange(count)

    def named(tallies, turn):
        used = int((tallies > 0).sum())
        fixed = max(1, used // 4)
        passed = fixed + (places - fixed + turn * (used - fixed)) % max(1, count - fixed)
        return jnp.zeros((count,), jnp.int32).at[ranking[jnp.where(places < fixed, places, passed)]].set(jnp.asarray(tallies, jnp.int32))

    tallies = jnp.where(number % 4 == 0, named(heavy_load, number // 4), named(common, number - number // 4 - 1))
    mixed = jax.random.permutation(jax.random.fold_in(own, 3), count)
    giver, sink = mixed[0:count // 2 * 2:2], mixed[1:count // 2 * 2:2]
    slack = jnp.minimum(tallies[giver] - 1, reach - tallies[sink]) // 2
    slack = jnp.where((giver == ranking[0]) | (sink == ranking[0]) | (tallies[sink] == 0), 0, jnp.maximum(slack, 0))
    passed = jax.random.randint(jax.random.fold_in(own, 4), (count // 2,), 0, 1 << 20) % (slack + 1)
    tallies = tallies.at[giver].add(-passed).at[sink].add(passed)
    labels = jnp.searchsorted(jnp.cumsum(tallies), jnp.arange(rows * top), side="right").astype(jnp.int32)
    table = labels.reshape(top, rows).T
    table = table[jax.random.permutation(jax.random.fold_in(own, 1), rows)]
    turn = jax.random.randint(jax.random.fold_in(own, 2), (rows, 1), 0, top)
    return jnp.take_along_axis(table, (jnp.arange(top)[None, :] + turn) % top, axis=1)


def shares(amount, total, limit, skew, full):
    weights = [(1 << 20) // math.isqrt(grade ** skew) + 1 for grade in range(1, amount + 1)]
    largest = limit if full else min(limit, max(-(-total // amount), total * weights[0] // sum(weights)))
    least = 1 if total - largest >= amount - 1 else 0
    given, spare = [largest] + [least] * (amount - 1), total - largest - least * (amount - 1)
    while spare > 0:
        candidates = [i for i in range(1, amount) if given[i] < largest] or [i for i in range(1, amount) if given[i] < limit]
        mass, left = sum([weights[i] for i in candidates]), spare
        for i in candidates:
            extra = min(limit - given[i], max(1, left * weights[i] // mass), spare)
            given[i] = given[i] + extra
            spare = spare - extra
    return np.array(given)


def normal_values(own_key, dims, deviation, most, cuts=(), kind=jnp.bfloat16):
    loudness = level_of(own_key, dims, cuts, -0.22, 0.18) if cuts else 1.0
    values = jax.random.normal(own_key, dims, jnp.float32) * deviation * loudness
    return jnp.minimum(jnp.maximum(values, -most), most).astype(kind)


def setup_inputs(seed: int = 0) -> dict:
    keys = jax.random.split(jax.random.key(seed), 10)
    weights = normal_values(keys[0], (REPLICAS, 3, EXPERTS * FF, D), D ** -0.5, 0.125, ((0, 32), (2, 16)))
    tokens = normal_values(keys[1], (REPLICAS, TOKENS, D), 1.0, 6.0, ((0, 32), (1, 16)))
    cotangent = normal_values(keys[2], (REPLICAS, TOKENS, D), 1.0, 6.0, ((0, 32), (1, 16)))
    routes_keys = jax.random.split(jax.random.fold_in(keys[3], 1), REPLICAS * TOKENS // TOK_DEV)
    routes_turns = jax.random.permutation(jax.random.fold_in(keys[3], 3), REPLICAS * TOKENS // TOK_DEV)
    routes = jax.vmap(lambda own, number: shared_out(jax.random.fold_in(keys[3], 2), own, number, TOK_DEV, EXPERTS, TOP, CAP, 1))(routes_keys, routes_turns).reshape((REPLICAS, TOKENS, TOP))
    gate_weights = jnp.clip(0.25 + 0.75 * jax.random.uniform(keys[4], (REPLICAS, TOKENS, TOP), jnp.float32) ** level_of(keys[4], (REPLICAS, TOKENS, TOP), ((0, 32), (1, 16)), -0.2, 0.2), 0.25, 1.0)
    next_tokens = normal_values(keys[5], (REPLICAS, TOKENS, D), 1.0, 6.0, ((0, 32), (1, 16)))
    next_routes_keys = jax.random.split(jax.random.fold_in(keys[6], 1), REPLICAS * TOKENS // TOK_DEV)
    next_routes_turns = jax.random.permutation(jax.random.fold_in(keys[6], 3), REPLICAS * TOKENS // TOK_DEV)
    next_routes = jax.vmap(lambda own, number: shared_out(jax.random.fold_in(keys[6], 2), own, number, TOK_DEV, EXPERTS, TOP, CAP, 1))(next_routes_keys, next_routes_turns).reshape((REPLICAS, TOKENS, TOP))
    next_gates = jnp.clip(0.25 + 0.75 * jax.random.uniform(keys[7], (REPLICAS, TOKENS, TOP), jnp.float32) ** level_of(keys[7], (REPLICAS, TOKENS, TOP), ((0, 32), (1, 16)), -0.2, 0.2), 0.25, 1.0)
    step_index = jax.random.randint(keys[8], (1,), 0, 64).astype(jnp.int32)
    return dict(weights=weights, tokens=tokens, cotangent=cotangent, routes=routes, gate_weights=gate_weights, next_tokens=next_tokens, next_routes=next_routes, next_gates=next_gates, step_index=step_index)


epsilon = 1e-06
contract_last = (((1,), (1,)), ((), ()))

def step_rate():
    return 2.0 / math.sqrt(D * N_EXPERT * CAP)

def sigmoid_slope(values):
    logistic = jax.nn.sigmoid(values)
    return logistic * (1.0 + values * (1.0 - logistic))

def assign_slots(block_routes):
    onehot = (block_routes[..., None] == jnp.arange(EXPERTS, dtype=jnp.int32)).astype(jnp.int32)
    before = jnp.cumsum(onehot, axis=1) - onehot
    return lax.optimization_barrier(jnp.sum(before * onehot, axis=-1)).astype(jnp.int32)

def to_buffers(rows_in, block_routes, slots):
    sources = rows_in.shape[0]
    source_ids = jnp.broadcast_to(jnp.arange(sources, dtype=jnp.int32)[:, None], block_routes.shape)
    empty = jnp.zeros((EXPERTS, sources, CAP, rows_in.shape[-1]), rows_in.dtype)
    filled = empty.at[block_routes, source_ids, slots].set(rows_in)
    return filled.reshape(EXPERTS, sources * CAP, rows_in.shape[-1])

def replica_update(packed):
    layer, inputs, cotangent, routes, gate_weights = packed
    block_routes = routes.reshape(N_EXPERT, TOK_DEV * TOP)
    slots = assign_slots(block_routes)
    token_rows = jnp.repeat(inputs, TOP, axis=0).reshape(N_EXPERT, TOK_DEV * TOP, D)
    scaled = (gate_weights[:, :, None] * cotangent[:, None, :].astype(jnp.float32)).astype(jnp.bfloat16)
    scaled = scaled.reshape(N_EXPERT, TOK_DEV * TOP, D)
    gathered = to_buffers(token_rows, block_routes, slots)
    upstream = to_buffers(scaled, block_routes, slots)
    pieces = []
    for expert in range(EXPERTS):
        w_gate = layer[0][expert * FF:(expert + 1) * FF, :]
        w_up = layer[1][expert * FF:(expert + 1) * FF, :]
        w_down = layer[2][expert * FF:(expert + 1) * FF, :]
        rows_x = gathered[expert]
        rows_d = upstream[expert]
        pre_gate = lax.dot_general(rows_x, w_gate, contract_last, preferred_element_type=jnp.float32)
        pre_up = lax.dot_general(rows_x, w_up, contract_last, preferred_element_type=jnp.float32)
        active = jax.nn.silu(pre_gate)
        hidden = (active * pre_up).astype(jnp.bfloat16)
        back = lax.dot_general(rows_d, w_down, contract_last, preferred_element_type=jnp.float32)
        d_gate = (back * pre_up * sigmoid_slope(pre_gate)).astype(jnp.bfloat16)
        d_up = (back * active).astype(jnp.bfloat16)
        g_gate = jnp.dot(d_gate.T, rows_x, preferred_element_type=jnp.float32)
        g_up = jnp.dot(d_up.T, rows_x, preferred_element_type=jnp.float32)
        g_down = jnp.dot(hidden.T, rows_d, preferred_element_type=jnp.float32)
        pieces.append(jnp.stack([g_gate, g_up, g_down]))
    grads = jnp.concatenate(pieces, axis=1).astype(jnp.bfloat16)
    return (layer.astype(jnp.float32) - step_rate() * grads.astype(jnp.float32)).astype(jnp.bfloat16)

def replica_forward(packed):
    layer, inputs, routes, gate_weights = packed
    block_routes = routes.reshape(N_EXPERT, TOK_DEV * TOP)
    slots = assign_slots(block_routes)
    token_rows = jnp.repeat(inputs, TOP, axis=0).reshape(N_EXPERT, TOK_DEV * TOP, D)
    gathered = to_buffers(token_rows, block_routes, slots)
    split_count = N_EXPERT // EXPERTS
    piece_width = FF // split_count
    outputs = []
    for expert in range(EXPERTS):
        w_gate = layer[0][expert * FF:(expert + 1) * FF, :]
        w_up = layer[1][expert * FF:(expert + 1) * FF, :]
        w_down = layer[2][expert * FF:(expert + 1) * FF, :]
        rows_x = gathered[expert]
        pre_gate = lax.dot_general(rows_x, w_gate, contract_last, preferred_element_type=jnp.float32)
        pre_up = lax.dot_general(rows_x, w_up, contract_last, preferred_element_type=jnp.float32)
        hidden = (jax.nn.silu(pre_gate) * pre_up).astype(jnp.bfloat16)
        total = jnp.zeros((rows_x.shape[0], D), jnp.float32)
        for member in range(split_count):
            lower = member * piece_width
            partial_out = jnp.dot(hidden[:, lower:lower + piece_width], w_down[lower:lower + piece_width, :], preferred_element_type=jnp.float32).astype(jnp.bfloat16)
            partial_out = lax.optimization_barrier(partial_out)
            total = total + partial_out.astype(jnp.float32)
        outputs.append(total)
    combined = jnp.stack(outputs).reshape(EXPERTS, N_EXPERT, CAP, D)
    source_ids = jnp.broadcast_to(jnp.arange(N_EXPERT, dtype=jnp.int32)[:, None], block_routes.shape)
    picked = combined[block_routes, source_ids, slots].reshape(TOKENS, TOP, D)
    mixed = lax.optimization_barrier(jnp.sum(picked * gate_weights[:, :, None], axis=1))
    scales = lax.optimization_barrier(jnp.max(jnp.abs(mixed), axis=1))
    codes = (mixed / (scales[:, None] + epsilon)).astype(jnp.bfloat16)
    return (codes, scales)

def reference(weights, tokens, cotangent, routes, gate_weights, next_tokens, next_routes, next_gates, step_index):
    updated = lax.map(replica_update, (weights, tokens, cotangent, routes, gate_weights))
    levels = min(4, N_REPLICA.bit_length() - 1)
    gossip_level = (step_index[0] % levels).astype(jnp.int32)
    distance = jnp.left_shift(jnp.int32(1), gossip_level).astype(jnp.int32)
    partners = jnp.bitwise_xor(jnp.arange(N_REPLICA, dtype=jnp.int32), distance).astype(jnp.int32)

    def average_one(replica):
        mine = updated[replica].astype(jnp.float32)
        theirs = updated[partners[replica]].astype(jnp.float32)
        return ((mine + theirs) * 0.5).astype(jnp.bfloat16)
    averaged = lax.map(average_one, jnp.arange(N_REPLICA, dtype=jnp.int32))
    token_codes, token_scales = lax.map(replica_forward, (averaged, next_tokens, next_routes, next_gates))
    return (token_codes, token_scales)
```

```python
import functools
import math

import jax
import jax.numpy as jnp
from jax import lax
from jax.experimental import pallas as pl
from jax.experimental.pallas import tpu as pltpu
from jax.sharding import PartitionSpec as P

D = 2048
EXPERTS = 4
CAP = 44
ROWS = 48
TOK = 128
HID = 192
CHIPS = 8
LEVELS = 4
COLS = 512
CHUNKS = D // COLS
GROUP = 4 * ROWS
RATE = 2.0 / math.sqrt(D * 16 * CAP)
epsilon = 1e-06
MESH = pl.DeviceIdType.MESH
contract_last = (((1,), (1,)), ((), ()))
contract_rows = (((0,), (0,)), ((), ()))


def dot(a, b):
    return jnp.dot(a, b, preferred_element_type=jnp.float32)


def dot_last(a, b):
    return lax.dot_general(a, b, contract_last, preferred_element_type=jnp.float32)


def one_hot_of(routes):
    lane = lax.broadcasted_iota(jnp.int32, (TOK, TOK), 1)
    row = lax.broadcasted_iota(jnp.int32, (TOK, TOK), 0)
    expert = routes.astype(jnp.int32)
    named = lane == expert
    earlier = (lane < row).astype(jnp.bfloat16)
    before = dot(earlier, named.astype(jnp.bfloat16))
    slot = jnp.sum(jnp.where(named, before, 0.0), axis=1, keepdims=True)
    target = expert * ROWS + slot.astype(jnp.int32)
    place = lax.broadcasted_iota(jnp.int32, (TOK, EXPERTS * ROWS), 1)
    return (place == target).astype(jnp.float32)


def place_rows(one_hot, rows, out_ref):
    table = one_hot.T.astype(jnp.bfloat16)
    for c in range(CHUNKS):
        cols = pl.ds(c * COLS, COLS)
        placed = dot(table, rows(cols)).astype(jnp.bfloat16)
        out_ref[:, :, cols] = placed.reshape(EXPERTS, ROWS, COLS)


def kernel(
    level,
    aux_ref,
    tok_ref,
    cot_ref,
    nxt_ref,
    w_ref,
    codes_ref,
    scales_ref,
    xb,
    sb,
    nb,
    rx,
    rs,
    rn,
    gate_t,
    up_t,
    d_t,
    own,
    theirs,
    acc,
    hid,
    hid_in,
    down,
    out,
    ret,
    mixed,
    table,
    x_send,
    x_recv,
    s_send,
    s_recv,
    n_send,
    n_recv,
    g_send,
    g_recv,
    h_send,
    h_recv,
    d_send,
    d_recv,
    o_send,
    o_recv,
):
    r = lax.axis_index("replica")
    e = lax.axis_index("expert")
    y = lax.div(e, 2)
    k = lax.rem(e, 2)
    side = 2 * lax.rem(y, 2) - 1
    mine = lax.div(y, 2)

    def chip(hops):
        return lax.rem(y + side * hops + 2 * CHIPS, CHIPS)

    def same_core(hops):
        return (r, chip(hops) * 2 + k)

    def other_core(hops):
        return (r, chip(hops) * 2 + 1 - k)

    def expert_at(hops):
        return lax.div(chip(hops), 2)

    apart = 1 << level
    partner = (r + apart * (1 - 2 * lax.rem(lax.div(r, apart), 2)), e)

    def remote(src, dst, send, recv, to):
        copy = pltpu.make_async_remote_copy(
            src_ref=src, dst_ref=dst, send_sem=send, recv_sem=recv, device_id=to, device_id_type=MESH
        )
        return copy

    started = []

    def start(src, dst, send, recv, to):
        copy = remote(src, dst, send, recv, to)
        copy.start()
        started.append(copy)

    def arrived(dst, send, recv):
        remote(dst, dst, send, recv, other_core(0)).wait_recv()

    barrier = pltpu.get_barrier_semaphore()
    peers = [same_core(h) for h in (1, 2, 3, -1, -2)] + [other_core(0), other_core(-1), partner]
    for peer in peers:
        pl.semaphore_signal(barrier, inc=1, device_id=peer, device_id_type=MESH)

    def place(lane, slot):
        return (lane * 2 + slot // 4, slot % 4)

    def dispatch(block, rows, send, recv):
        for n, (slot, hops) in enumerate(((1, 1), (3, 3), (2, -2), (4, -1))):
            start(block.at[expert_at(hops)], rows.at[place(0, slot)], send.at[n], recv.at[slot], same_core(hops))
        start(block.at[mine], rows.at[place(1, 0)], send.at[4], recv.at[8], other_core(0))
        rows[place(0, 0)] = block[mine]

    def take(rows, slot, send, recv):
        here = rows.at[place(0, slot)]
        arrived(here, send.at[0], recv.at[slot])
        if slot < 4:
            start(here, rows.at[place(0, slot + 4)], send.at[11 + slot], recv.at[slot + 4], same_core(-1))
        start(here, rows.at[place(1, slot)], send.at[4 + slot], recv.at[8 + slot], other_core(0))

    def take_lane(rows, slot, send, recv):
        arrived(rows.at[place(1, slot)], send.at[0], recv.at[8 + slot])

    hot = one_hot_of(aux_ref[:, 0:1])
    place_rows(hot, lambda cols: tok_ref[:, cols], xb)
    pl.semaphore_wait(barrier, len(peers))
    dispatch(xb, rx, x_send, x_recv)
    gates = aux_ref[:, 1:2]
    place_rows(hot, lambda cols: (gates * cot_ref[:, cols].astype(jnp.float32)).astype(jnp.bfloat16), sb)
    dispatch(sb, rs, s_send, s_recv)
    hot_next = one_hot_of(aux_ref[:, 2:3])
    place_rows(hot_next, lambda cols: nxt_ref[:, cols], nb)
    table[...] = hot_next.astype(jnp.bfloat16)

    def group(ref, q, cols):
        return ref[q, :, :, cols].reshape(GROUP, COLS)

    def forward_x(half):
        for slot in range(4 * half, 4 * half + 4):
            take_lane(rx, slot, x_send, x_recv)

        def body(lane, carry):
            q = lane * 2 + half
            for j, ref in ((0, gate_t), (1, up_t)):
                total = jnp.zeros((HID, GROUP), jnp.float32)
                for c in range(CHUNKS):
                    cols = pl.ds(c * COLS, COLS)
                    total += dot_last(w_ref[j, :, cols], group(rx, q, cols))
                ref[q] = total
            return carry

        lax.fori_loop(0, 2, body, 0)

    def backward_s(half):
        for slot in range(4 * half, 4 * half + 4):
            take_lane(rs, slot, s_send, s_recv)

        def body(lane, carry):
            q = lane * 2 + half
            back = jnp.zeros((HID, GROUP), jnp.float32)
            for c in range(CHUNKS):
                cols = pl.ds(c * COLS, COLS)
                back += dot_last(w_ref[2, :, cols], group(rs, q, cols))
            gate = gate_t[q]
            up = up_t[q]
            logistic = jax.nn.sigmoid(gate)
            active = gate * logistic
            d_t[0, q] = (back * up * (logistic * (1.0 + gate * (1.0 - logistic)))).astype(jnp.bfloat16)
            d_t[1, q] = (back * active).astype(jnp.bfloat16)
            d_t[2, q] = (active * up).astype(jnp.bfloat16)
            return carry

        lax.fori_loop(0, 2, body, 0)

    for slot in (1, 2, 3, 4):
        take(rx, slot, x_send, x_recv)
    forward_x(0)
    for slot in (1, 2, 3):
        take(rs, slot, s_send, s_recv)
    for slot in (5, 6, 7):
        take(rx, slot, x_send, x_recv)
    forward_x(1)
    take(rs, 4, s_send, s_recv)
    backward_s(0)
    for slot in (5, 6, 7):
        take(rs, slot, s_send, s_recv)
    dispatch(nb, rn, n_send, n_recv)
    backward_s(1)

    def update(j, c, index):
        cols = pl.ds(c * COLS, COLS)
        rows = rs if j == 2 else rx
        grad = jnp.zeros((HID, COLS), jnp.float32)
        for q in range(4):
            grad += dot(d_t[j, q], group(rows, q, cols))
        grad = grad.astype(jnp.bfloat16).astype(jnp.float32)
        own[index] = (w_ref[j, :, cols].astype(jnp.float32) - RATE * grad).astype(jnp.bfloat16)
        start(own.at[index], theirs.at[index], g_send.at[index], g_recv.at[index], partner)

    for c in range(CHUNKS):
        update(0, c, 2 * c)
        update(1, c, 2 * c + 1)
    for slot in (1, 2, 3):
        take(rn, slot, n_send, n_recv)
    for c in range(CHUNKS):
        update(2, c, 2 * CHUNKS + c)
    for slot in (4, 5, 6, 7):
        take(rn, slot, n_send, n_recv)
    for slot in range(8):
        take_lane(rn, slot, n_send, n_recv)

    def averaged(index):
        arrived(theirs.at[index], g_send.at[index], g_recv.at[index])
        both = own[index].astype(jnp.float32) + theirs[index].astype(jnp.float32)
        return (both * 0.5).astype(jnp.bfloat16)

    acc[...] = jnp.zeros_like(acc)
    for c in range(CHUNKS):
        cols = pl.ds(c * COLS, COLS)
        for j in range(2):
            weight = averaged(2 * c + j)
            for q in range(4):
                acc[j, q] += dot_last(group(rn, q, cols), weight)
    for q in range(4):
        gate = acc[0, q]
        value = (gate * jax.nn.sigmoid(gate) * acc[1, q]).astype(jnp.bfloat16)
        hid[q] = value.reshape(4, ROWS, HID)

    for n, (q, to) in enumerate(((2, other_core(0)), (1, same_core(-1)), (3, other_core(-1)))):
        start(hid.at[q], hid_in.at[n], h_send.at[n], h_recv.at[n], to)

    def down_start(c):
        down[0, c] = averaged(2 * CHUNKS + c)
        start(down.at[0, c], down.at[2, c], d_send.at[1, c], d_recv.at[1, c], same_core(-1))
        start(down.at[0, c], down.at[1, c], d_send.at[0, c], d_recv.at[0, c], other_core(0))

    def down_finish(c):
        arrived(down.at[2, c], d_send.at[1, c], d_recv.at[1, c])
        start(down.at[2, c], down.at[3, c], d_send.at[2, c], d_recv.at[2, c], other_core(0))
        arrived(down.at[1, c], d_send.at[0, c], d_recv.at[0, c])
        if c == 0:
            for n in range(3):
                arrived(hid_in.at[n], h_send.at[n], h_recv.at[n])
        total = dot(hid[0].reshape(GROUP, HID), down[0, c])
        total += dot(hid_in[0].reshape(GROUP, HID), down[1, c])
        total += dot(hid_in[1].reshape(GROUP, HID), down[2, c])
        arrived(down.at[3, c], d_send.at[2, c], d_recv.at[2, c])
        total += dot(hid_in[2].reshape(GROUP, HID), down[3, c])
        out[c] = total.astype(jnp.bfloat16).reshape(4, ROWS, COLS)
        for slot in (3, 2, 1):
            start(
                out.at[c, slot],
                ret.at[mine, c],
                o_send.at[slot - 1, c],
                o_recv.at[slot - 1, c],
                same_core(slot),
            )
        ret[mine, c] = out[c, 0]

    down_start(0)
    for c in range(1, CHUNKS):
        down_start(c)
        down_finish(c - 1)
    down_finish(CHUNKS - 1)

    next_gates = aux_ref[:, 3:4]
    largest = jnp.zeros((TOK, 1), jnp.float32)
    for c in range(CHUNKS):
        for slot, hops in ((1, 1), (2, -2), (3, 3)):
            arrived(ret.at[expert_at(hops), c], o_send.at[slot - 1, c], o_recv.at[slot - 1, c])
        value = dot(table[...], ret[:, c].reshape(EXPERTS * ROWS, COLS)) * next_gates
        mixed[c] = value
        largest = jnp.maximum(largest, jnp.max(jnp.abs(value), axis=1, keepdims=True))
    scales_ref[...] = largest
    for c in range(CHUNKS):
        codes_ref[:, pl.ds(c * COLS, COLS)] = (mixed[c] / (largest + epsilon)).astype(jnp.bfloat16)

    for copy in started:
        copy.wait_send()


def step(level, aux, tokens, cotangent, next_tokens, weights):
    vmem = pl.BlockSpec(memory_space=pltpu.VMEM)
    bf16, f32 = jnp.bfloat16, jnp.float32
    dma = pltpu.SemaphoreType.DMA
    block = pltpu.VMEM((EXPERTS, ROWS, D), bf16)
    rows = pltpu.VMEM((4, 4, ROWS, D), bf16)
    return pl.pallas_call(
        functools.partial(kernel, level),
        out_shape=(
            jax.ShapeDtypeStruct((TOK, D), bf16),
            jax.ShapeDtypeStruct((TOK, 1), f32),
        ),
        in_specs=[vmem] * 5,
        out_specs=(vmem, vmem),
        scratch_shapes=[
            block,
            block,
            block,
            rows,
            rows,
            rows,
            pltpu.VMEM((4, HID, GROUP), f32),
            pltpu.VMEM((4, HID, GROUP), f32),
            pltpu.VMEM((3, 4, HID, GROUP), bf16),
            pltpu.VMEM((3 * CHUNKS, HID, COLS), bf16),
            pltpu.VMEM((3 * CHUNKS, HID, COLS), bf16),
            pltpu.VMEM((2, 4, GROUP, HID), f32),
            pltpu.VMEM((4, 4, ROWS, HID), bf16),
            pltpu.VMEM((3, 4, ROWS, HID), bf16),
            pltpu.VMEM((4, CHUNKS, HID, COLS), bf16),
            pltpu.VMEM((CHUNKS, 4, ROWS, COLS), bf16),
            pltpu.VMEM((EXPERTS, CHUNKS, ROWS, COLS), bf16),
            pltpu.VMEM((CHUNKS, TOK, COLS), f32),
            pltpu.VMEM((TOK, EXPERTS * ROWS), bf16),
            dma((15,)),
            dma((16,)),
            dma((15,)),
            dma((16,)),
            dma((15,)),
            dma((16,)),
            dma((3 * CHUNKS,)),
            dma((3 * CHUNKS,)),
            dma((3,)),
            dma((3,)),
            dma((3, CHUNKS)),
            dma((3, CHUNKS)),
            dma((3, CHUNKS)),
            dma((3, CHUNKS)),
        ],
        compiler_params=pltpu.CompilerParams(
            collective_id=level, has_side_effects=True, vmem_limit_bytes=48 * 2**20
        ),
        name=f"step_{level}",
    )(aux, tokens, cotangent, next_tokens, weights)


def local(
    weights,
    tokens,
    cotangent,
    routes,
    gate_weights,
    next_tokens,
    next_routes,
    next_gates,
    step_index,
):
    aux = jnp.concatenate(
        [routes[0].astype(jnp.float32), gate_weights[0], next_routes[0].astype(jnp.float32), next_gates[0]],
        axis=1,
    )
    branches = [functools.partial(step, level) for level in range(LEVELS)]
    codes, scales = lax.switch(
        step_index[0] % LEVELS, branches, aux, tokens[0], cotangent[0], next_tokens[0], weights[0]
    )
    return (codes[None], scales.reshape(1, TOK))


def solution(mesh):
    placed = (
        P("replica", None, "expert", None),
        P("replica", "expert", None),
        P("replica", "expert", None),
        P("replica", "expert", None),
        P("replica", "expert", None),
        P("replica", "expert", None),
        P("replica", "expert", None),
        P("replica", "expert", None),
        P(),
    )
    return jax.shard_map(
        local,
        mesh=mesh,
        in_specs=placed,
        out_specs=(P("replica", "expert", None), P("replica", "expert")),
        check_vma=False,
    )
```

```python
import functools
import math

import jax
import jax.numpy as jnp
from jax import lax
from jax.experimental import pallas as pl
from jax.experimental.pallas import tpu as pltpu
from jax.sharding import PartitionSpec as P

D = 2048
EXPERTS = 4
CAP = 44
ROWS = 48
TOK = 128
HID = 192
CHIPS = 8
LEVELS = 4
COLS = 512
CHUNKS = D // COLS
GROUP = 4 * ROWS
KINDS = 3
EARLY = (3, 2, 2, 3)
RATE = 2.0 / math.sqrt(D * 16 * CAP)
epsilon = 1e-06
MESH = pl.DeviceIdType.MESH
contract_last = (((1,), (1,)), ((), ()))
contract_rows = (((0,), (0,)), ((), ()))


def dot(a, b):
    return jnp.dot(a, b, preferred_element_type=jnp.float32)


def dot_last(a, b):
    return lax.dot_general(a, b, contract_last, preferred_element_type=jnp.float32)


def column(row):
    lane = lax.broadcasted_iota(jnp.int32, (TOK, TOK), 1)
    across = lax.broadcasted_iota(jnp.int32, (TOK, TOK), 0)
    return jnp.sum(jnp.where(lane == across, row, 0.0), axis=1, keepdims=True)


def one_hot_of(routes):
    lane = lax.broadcasted_iota(jnp.int32, (TOK, TOK), 1)
    across = lax.broadcasted_iota(jnp.int32, (TOK, TOK), 0)
    earlier = (across < lane).astype(jnp.bfloat16)
    named = lax.broadcasted_iota(jnp.int32, (16, TOK), 0) == routes
    before = dot(named.astype(jnp.bfloat16), earlier)
    slot = jnp.sum(jnp.where(named, before, 0.0), axis=0, keepdims=True)
    target = routes * ROWS + slot.astype(jnp.int32)
    place = lax.broadcasted_iota(jnp.int32, (EXPERTS * ROWS, TOK), 0)
    return (place == target).astype(jnp.float32)


def columns(c):
    return pl.ds(pl.multiple_of(c * COLS, COLS), COLS)


def kernel(
    level,
    routes_ref,
    gates_ref,
    next_routes_ref,
    next_gates_ref,
    tok_hbm,
    cot_hbm,
    nxt_hbm,
    w_hbm,
    codes_ref,
    scales_ref,
    held,
    w_ref,
    block,
    rows,
    gate_t,
    up_t,
    back_t,
    d_t,
    own,
    theirs,
    acc,
    hid,
    hid_in,
    down,
    out,
    ret,
    mixed,
    table,
    l_sem,
    x_send,
    x_recv,
    g_send,
    g_recv,
    h_send,
    h_recv,
    d_send,
    d_recv,
    o_send,
    o_recv,
):
    r = lax.axis_index("replica")
    e = lax.axis_index("expert")
    y = lax.div(e, 2)
    k = lax.rem(e, 2)
    side = 2 * lax.rem(y, 2) - 1
    mine = lax.div(y, 2)

    def chip(hops):
        return lax.rem(y + side * hops + 2 * CHIPS, CHIPS)

    def same_core(hops):
        return (r, chip(hops) * 2 + k)

    def other_core(hops):
        return (r, chip(hops) * 2 + 1 - k)

    def expert_at(hops):
        return lax.div(chip(hops), 2)

    apart = 1 << level
    partner = (r + apart * (1 - 2 * lax.rem(lax.div(r, apart), 2)), e)

    def remote(src, dst, send, recv, to):
        return pltpu.make_async_remote_copy(
            src_ref=src, dst_ref=dst, send_sem=send, recv_sem=recv, device_id=to, device_id_type=MESH
        )

    barrier = pltpu.get_barrier_semaphore()
    peers = [same_core(h) for h in (1, 2, 3, -1, -2)] + [other_core(0), other_core(-1), partner]
    for peer in peers:
        pl.semaphore_signal(barrier, inc=1, device_id=peer, device_id_type=MESH)
    def over(first, last, body):
        def run(p, carry):
            body(p)
            return carry

        lax.fori_loop(first, last, run, 0)

    def load_tokens(c):
        return pltpu.make_async_copy(tok_hbm.at[:, columns(c)], held.at[0, :, columns(c)], l_sem.at[c])

    over(0, CHUNKS, lambda c: load_tokens(c).start())
    loads = [
        pltpu.make_async_copy(src, dst, l_sem.at[CHUNKS + n])
        for n, (src, dst) in enumerate(((cot_hbm, held.at[1]), (nxt_hbm, held.at[2]), (w_hbm, w_ref)))
    ]
    for load in loads:
        load.start()
    early_chunks = EARLY[level]

    def place(p, lane, slot):
        return rows.at[p, lane * 2 + slot // 4, slot % 4]

    def direct(p):
        copies = [
            remote(
                block.at[p, expert_at(hops)], place(p, 0, slot), x_send.at[p, n], x_recv.at[p, slot], same_core(hops)
            )
            for n, (slot, hops) in enumerate(((1, 1), (3, 3), (2, -2), (4, -1)))
        ]
        return copies + [
            remote(block.at[p, mine], place(p, 1, 0), x_send.at[p, 4], x_recv.at[p, 8], other_core(0))
        ]

    def relay(p, slot):
        return remote(
            place(p, 0, slot), place(p, 0, slot + 4), x_send.at[p, 11 + slot], x_recv.at[p, slot + 4], same_core(-1)
        )

    def forward(p, slot):
        return remote(
            place(p, 0, slot), place(p, 1, slot), x_send.at[p, 4 + slot], x_recv.at[p, 8 + slot], other_core(0)
        )

    def dispatch(p):
        for copy in direct(p):
            copy.start()
        rows[p, 0, 0] = block[p, mine]

    def takes(p, slots):
        for slot in slots:
            remote(
                place(p, 0, slot), place(p, 0, slot), x_send.at[p, 0], x_recv.at[p, slot], other_core(0)
            ).wait_recv()
            if slot < 4:
                relay(p, slot).start()
            forward(p, slot).start()

    def take_lane(p, slots):
        for slot in slots:
            remote(
                place(p, 1, slot), place(p, 1, slot), x_send.at[p, 0], x_recv.at[p, 8 + slot], other_core(0)
            ).wait_recv()

    def place_rows(p, hot, scale):
        value = held[p // CHUNKS, :, columns(p % CHUNKS)]
        if scale is not None:
            value = (scale * value.astype(jnp.float32)).astype(jnp.bfloat16)
        block[p] = dot(hot, value).astype(jnp.bfloat16).reshape(EXPERTS, ROWS, COLS)

    hot = one_hot_of(routes_ref[...]).astype(jnp.bfloat16)
    load_tokens(0).wait()
    place_rows(0, hot, None)
    pl.semaphore_wait(barrier, len(peers))
    dispatch(0)

    def place_x(p):
        load_tokens(p).wait()
        place_rows(p, hot, None)
        dispatch(p)

    over(1, 4, place_x)
    loads[0].wait()
    gates = column(gates_ref[...])
    over(4, 8, lambda p: place_rows(p, hot, gates))
    dispatch(4)
    hot_next = one_hot_of(next_routes_ref[...])
    hot_next_rows = hot_next.astype(jnp.bfloat16)
    loads[1].wait()
    over(8, 12, lambda p: place_rows(p, hot_next_rows, None))
    table[...] = hot_next.T.astype(jnp.bfloat16)
    loads[2].wait()

    def group(kind, q, c):
        return rows[kind * CHUNKS + c, q].reshape(GROUP, COLS)

    def forward_x(q):
        gate_t[q] = jnp.zeros((HID, GROUP), jnp.float32)
        up_t[q] = jnp.zeros((HID, GROUP), jnp.float32)
        back_t[q] = jnp.zeros((HID, GROUP), jnp.float32)

        def body(c):
            value = group(0, q, c)
            gate_t[q] += dot_last(w_ref[0, :, columns(c)], value)
            up_t[q] += dot_last(w_ref[1, :, columns(c)], value)

        over(0, CHUNKS, body)
        gate = gate_t[q]
        d_t[2, q] = (gate * jax.nn.sigmoid(gate) * up_t[q]).astype(jnp.bfloat16)

    def backward(q, c):
        back_t[q] += dot_last(w_ref[2, :, columns(c)], group(1, q, c))

    def slopes(q):
        back = back_t[q]
        gate = gate_t[q]
        up = up_t[q]
        logistic = jax.nn.sigmoid(gate)
        d_t[0, q] = (back * up * (logistic * (1.0 + gate * (1.0 - logistic)))).astype(jnp.bfloat16)
        d_t[1, q] = (back * (gate * logistic)).astype(jnp.bfloat16)

    def exchange(index):
        return remote(own.at[index], theirs.at[index], g_send.at[index], g_recv.at[index], partner)

    def update(j, c, index):
        cols = columns(c)
        kind = j // 2
        grad = jnp.zeros((HID, COLS), jnp.float32)
        for q in range(4):
            grad += dot(d_t[j, q], group(kind, q, c))
        grad = grad.astype(jnp.bfloat16).astype(jnp.float32)
        own[index] = (w_ref[j, :, cols].astype(jnp.float32) - RATE * grad).astype(jnp.bfloat16)
        exchange(index).start()

    def update_up(c):
        over(0, 2, lambda j: update(j, c, 2 * c + j))
        takes(8 + c, near)

    def update_down(c):
        update(2, c, 2 * CHUNKS + c)

    near, rest = (1, 2, 3), (4, 5, 6, 7)
    over(0, 4, lambda p: takes(p, near))
    dispatch(5)

    def forward_half(half):
        @pl.when(half == 1)
        def _():
            over(0, 4, lambda p: takes(p, rest))

        over(0, 4, lambda p: take_lane(p, [4 * half + n for n in range(4)]))
        over(0, 2, lambda lane: forward_x(2 * lane + half))
        takes(4 + half, near)
        dispatch(6 + half)

    over(0, 2, forward_half)

    def early(c):
        takes(c + 4, rest)
        take_lane(c + 4, range(8))

        @pl.when(c < early_chunks)
        def _():
            update_down(c)

        over(0, 4, lambda q: backward(q, c))

        @pl.when(c < 2)
        def _():
            takes(c + 6, near)

    over(0, 3, early)
    takes(7, rest)
    over(8, 12, dispatch)
    take_lane(7, range(8))

    def backward_last(q):
        backward(q, CHUNKS - 1)
        slopes(q)

    over(0, 4, backward_last)
    over(0, CHUNKS, update_up)
    over(early_chunks, CHUNKS, update_down)

    def averaged(index):
        exchange(index).wait_recv()
        both = own[index].astype(jnp.float32) + theirs[index].astype(jnp.float32)
        return (both * 0.5).astype(jnp.bfloat16)

    def to_core(c):
        return remote(down.at[0, c], down.at[1, c], d_send.at[0, c], d_recv.at[0, c], other_core(0))

    def to_pair(c):
        return remote(down.at[0, c], down.at[2, c], d_send.at[1, c], d_recv.at[1, c], same_core(-1))

    def pair_to_core(c):
        return remote(down.at[2, c], down.at[3, c], d_send.at[2, c], d_recv.at[2, c], other_core(0))

    def give_back(c, slot):
        return remote(
            out.at[c, slot], ret.at[mine, c], o_send.at[slot - 1, c], o_recv.at[slot - 1, c], same_core(slot)
        )

    def down_start(c):
        down[0, c] = averaged(2 * CHUNKS + c)
        to_pair(c).start()
        to_core(c).start()

    def down_relay(c):
        to_pair(c).wait_recv()
        pair_to_core(c).start()

    def down_finish(c):
        total = dot(hid[0].reshape(GROUP, HID), down[0, c])
        to_core(c).wait_recv()
        total += dot(hid_in[0].reshape(GROUP, HID), down[1, c])
        total += dot(hid_in[1].reshape(GROUP, HID), down[2, c])
        pair_to_core(c).wait_recv()
        total += dot(hid_in[2].reshape(GROUP, HID), down[3, c])
        out[c] = total.astype(jnp.bfloat16).reshape(4, ROWS, COLS)
        for slot in (3, 2, 1):
            give_back(c, slot).start()
        ret[mine, c] = out[c, 0]

    over(0, early_chunks, down_start)
    over(8, 12, lambda p: takes(p, rest))
    over(8, 12, lambda p: take_lane(p, range(8)))
    acc[...] = jnp.zeros_like(acc)

    def average_up(c, j):
        weight = averaged(2 * c + j)
        exchange(2 * c + j).wait_send()
        own[2 * c + j] = weight

    def forward_next(index):
        c, j = index // 2, index % 2
        average_up(c, j)

        def body(q):
            acc[j, q] += dot_last(group(2, q, c), own[index])

        over(0, 4, body)

    over(0, 2 * CHUNKS - 1, forward_next)
    over(0, early_chunks, down_relay)
    average_up(CHUNKS - 1, 1)

    def hidden(n):
        q, to = ((2, other_core(0)), (1, same_core(-1)), (3, other_core(-1)))[n]
        return remote(hid.at[q], hid_in.at[n], h_send.at[n], h_recv.at[n], to)

    def activate(q):
        gate = acc[0, q]
        up = acc[1, q] + dot_last(group(2, q, CHUNKS - 1), own[2 * CHUNKS - 1])
        value = (gate * jax.nn.sigmoid(gate) * up).astype(jnp.bfloat16)
        hid[q] = value.reshape(4, ROWS, HID)

    def activate_send(n):
        activate(3 - n)
        for when, copy in ((0, 2), (1, 0), (2, 1)):

            @pl.when(n == when)
            def _():
                hidden(copy).start()

    over(0, 4, activate_send)
    for n in range(3):
        hidden(n).wait_recv()

    def down_steps(c):
        if early_chunks == 3:

            @pl.when(c == 2)
            def _():
                down_start(3)

            @pl.when(c == 3)
            def _():
                down_relay(3)

        else:

            @pl.when(c >= 2)
            def _():
                down_start(c)
                down_relay(c)

        down_finish(c)

    over(0, CHUNKS, down_steps)

    next_gates = column(next_gates_ref[...])

    def mix(c, largest):
        for slot, hops in ((1, 1), (2, -2), (3, 3)):
            here = ret.at[expert_at(hops), c]
            remote(here, here, o_send.at[slot - 1, c], o_recv.at[slot - 1, c], other_core(0)).wait_recv()
        value = dot(table[...], ret[:, c].reshape(EXPERTS * ROWS, COLS)) * next_gates
        mixed[c] = value
        return jnp.maximum(largest, jnp.max(jnp.abs(value), axis=1, keepdims=True))

    largest = lax.fori_loop(0, CHUNKS, mix, jnp.zeros((TOK, 1), jnp.float32))
    inverse = 1.0 / (largest + epsilon)

    def code(c):
        codes_ref[:, columns(c)] = (mixed[c] * inverse).astype(jnp.bfloat16)

    over(0, CHUNKS, code)
    lane = lax.broadcasted_iota(jnp.int32, (TOK, TOK), 1)
    across = lax.broadcasted_iota(jnp.int32, (TOK, TOK), 0)
    scales_ref[...] = jnp.sum(jnp.where(lane == across, largest, 0.0), axis=0, keepdims=True)

    def rows_sent(p):
        for copy in direct(p) + [relay(p, slot) for slot in near] + [forward(p, slot) for slot in range(1, 8)]:
            copy.wait_send()

    def chunk_sent(c):
        exchange(2 * CHUNKS + c).wait_send()
        to_pair(c).wait_send()
        to_core(c).wait_send()
        pair_to_core(c).wait_send()
        for slot in near:
            give_back(c, slot).wait_send()

    over(0, KINDS * CHUNKS, rows_sent)
    for n in range(3):
        hidden(n).wait_send()
    over(0, CHUNKS, chunk_sent)


def step(level, routes, gates, next_routes, next_gates, tokens, cotangent, next_tokens, weights):
    vmem = pl.BlockSpec(memory_space=pltpu.VMEM)
    hbm = pl.BlockSpec(memory_space=pl.ANY)
    bf16, f32 = jnp.bfloat16, jnp.float32
    dma = pltpu.SemaphoreType.DMA
    return pl.pallas_call(
        functools.partial(kernel, level),
        out_shape=(
            jax.ShapeDtypeStruct((TOK, D), bf16),
            jax.ShapeDtypeStruct((1, TOK), f32),
        ),
        in_specs=[vmem] * 4 + [hbm] * 4,
        out_specs=(vmem, vmem),
        scratch_shapes=[
            pltpu.VMEM((3, TOK, D), bf16),
            pltpu.VMEM((3, HID, D), bf16),
            pltpu.VMEM((KINDS * CHUNKS, EXPERTS, ROWS, COLS), bf16),
            pltpu.VMEM((KINDS * CHUNKS, 4, 4, ROWS, COLS), bf16),
            pltpu.VMEM((4, HID, GROUP), f32),
            pltpu.VMEM((4, HID, GROUP), f32),
            pltpu.VMEM((4, HID, GROUP), f32),
            pltpu.VMEM((3, 4, HID, GROUP), bf16),
            pltpu.VMEM((3 * CHUNKS, HID, COLS), bf16),
            pltpu.VMEM((3 * CHUNKS, HID, COLS), bf16),
            pltpu.VMEM((2, 4, GROUP, HID), f32),
            pltpu.VMEM((4, 4, ROWS, HID), bf16),
            pltpu.VMEM((3, 4, ROWS, HID), bf16),
            pltpu.VMEM((4, CHUNKS, HID, COLS), bf16),
            pltpu.VMEM((CHUNKS, 4, ROWS, COLS), bf16),
            pltpu.VMEM((EXPERTS, CHUNKS, ROWS, COLS), bf16),
            pltpu.VMEM((CHUNKS, TOK, COLS), f32),
            pltpu.VMEM((TOK, EXPERTS * ROWS), bf16),
            dma((CHUNKS + 3,)),
            dma((KINDS * CHUNKS, 15)),
            dma((KINDS * CHUNKS, 16)),
            dma((3 * CHUNKS,)),
            dma((3 * CHUNKS,)),
            dma((3,)),
            dma((3,)),
            dma((3, CHUNKS)),
            dma((3, CHUNKS)),
            dma((3, CHUNKS)),
            dma((3, CHUNKS)),
        ],
        compiler_params=pltpu.CompilerParams(
            collective_id=level, has_side_effects=True, vmem_limit_bytes=48 * 2**20
        ),
        name=f"step_{level}",
    )(routes, gates, next_routes, next_gates, tokens, cotangent, next_tokens, weights)


def local(
    weights,
    tokens,
    cotangent,
    routes,
    gate_weights,
    next_tokens,
    next_routes,
    next_gates,
    step_index,
):
    branches = [functools.partial(step, level) for level in range(LEVELS)]
    codes, scales = lax.switch(
        step_index[0] % LEVELS,
        branches,
        routes.reshape(1, TOK),
        gate_weights.reshape(1, TOK),
        next_routes.reshape(1, TOK),
        next_gates.reshape(1, TOK),
        tokens[0],
        cotangent[0],
        next_tokens[0],
        weights[0],
    )
    return (codes[None], scales)


def solution(mesh):
    placed = (
        P("replica", None, "expert", None),
        P("replica", "expert", None),
        P("replica", "expert", None),
        P("replica", "expert", None),
        P("replica", "expert", None),
        P("replica", "expert", None),
        P("replica", "expert", None),
        P("replica", "expert", None),
        P(),
    )
    return jax.shard_map(
        local,
        mesh=mesh,
        in_specs=placed,
        out_specs=(P("replica", "expert", None), P("replica", "expert")),
        check_vma=False,
    )
```

```python
import functools
import math

import jax
import jax.numpy as jnp
from jax import lax
from jax.experimental import pallas as pl
from jax.experimental.pallas import tpu as pltpu
from jax.sharding import PartitionSpec as P

D = 2048
EXPERTS = 4
CAP = 44
ROWS = 48
TOK = 128
HID = 192
CHIPS = 8
LEVELS = 4
COLS = 512
CHUNKS = D // COLS
GROUP = 4 * ROWS
KINDS = 3
EARLY = (3, 2, 2, 3)
FINE = 256
FINES = D // FINE
SPLIT = COLS // FINE
RATE = 2.0 / math.sqrt(D * 16 * CAP)
epsilon = 1e-06
MESH = pl.DeviceIdType.MESH
contract_last = (((1,), (1,)), ((), ()))
contract_rows = (((0,), (0,)), ((), ()))


def dot(a, b):
    return jnp.dot(a, b, preferred_element_type=jnp.float32)


def dot_last(a, b):
    return lax.dot_general(a, b, contract_last, preferred_element_type=jnp.float32)


def column(row):
    lane = lax.broadcasted_iota(jnp.int32, (TOK, TOK), 1)
    across = lax.broadcasted_iota(jnp.int32, (TOK, TOK), 0)
    return jnp.sum(jnp.where(lane == across, row, 0.0), axis=1, keepdims=True)


def one_hot_of(routes):
    lane = lax.broadcasted_iota(jnp.int32, (TOK, TOK), 1)
    across = lax.broadcasted_iota(jnp.int32, (TOK, TOK), 0)
    earlier = (across < lane).astype(jnp.bfloat16)
    named = lax.broadcasted_iota(jnp.int32, (16, TOK), 0) == routes
    before = dot(named.astype(jnp.bfloat16), earlier)
    slot = jnp.sum(jnp.where(named, before, 0.0), axis=0, keepdims=True)
    target = routes * ROWS + slot.astype(jnp.int32)
    place = lax.broadcasted_iota(jnp.int32, (EXPERTS * ROWS, TOK), 0)
    return (place == target).astype(jnp.float32)


def columns(c):
    return pl.ds(pl.multiple_of(c * COLS, COLS), COLS)


def fine_columns(c):
    return pl.ds(pl.multiple_of(c * FINE, FINE), FINE)


def kernel(
    level,
    routes_ref,
    gates_ref,
    next_routes_ref,
    next_gates_ref,
    tok_hbm,
    cot_hbm,
    nxt_hbm,
    w_hbm,
    codes_ref,
    scales_ref,
    held,
    w_ref,
    block,
    rows,
    pre_t,
    back_t,
    d_t,
    own,
    theirs,
    own_down,
    their_down,
    acc,
    hid,
    hid_in,
    down,
    out,
    ret,
    mixed,
    table,
    l_sem,
    x_send,
    x_recv,
    g_send,
    g_recv,
    f_send,
    f_recv,
    h_send,
    h_recv,
    d_send,
    d_recv,
    o_send,
    o_recv,
):
    r = lax.axis_index("replica")
    e = lax.axis_index("expert")
    y = lax.div(e, 2)
    k = lax.rem(e, 2)
    side = 2 * lax.rem(y, 2) - 1
    mine = lax.div(y, 2)

    def chip(hops):
        return lax.rem(y + side * hops + 2 * CHIPS, CHIPS)

    def same_core(hops):
        return (r, chip(hops) * 2 + k)

    def other_core(hops):
        return (r, chip(hops) * 2 + 1 - k)

    def expert_at(hops):
        return lax.div(chip(hops), 2)

    apart = 1 << level
    partner = (r + apart * (1 - 2 * lax.rem(lax.div(r, apart), 2)), e)

    def remote(src, dst, send, recv, to):
        return pltpu.make_async_remote_copy(
            src_ref=src, dst_ref=dst, send_sem=send, recv_sem=recv, device_id=to, device_id_type=MESH
        )

    barrier = pltpu.get_barrier_semaphore()
    peers = [same_core(h) for h in (1, 2, 3, -1, -2)] + [other_core(0), other_core(-1), partner]
    for peer in peers:
        pl.semaphore_signal(barrier, inc=1, device_id=peer, device_id_type=MESH)
    def over(first, last, body):
        def run(p, carry):
            body(p)
            return carry

        lax.fori_loop(first, last, run, 0)

    def load_tokens(c):
        return pltpu.make_async_copy(tok_hbm.at[:, columns(c)], held.at[0, :, columns(c)], l_sem.at[c])

    over(0, CHUNKS, lambda c: load_tokens(c).start())
    loads = [
        pltpu.make_async_copy(src, dst, l_sem.at[CHUNKS + n])
        for n, (src, dst) in enumerate(((cot_hbm, held.at[1]), (nxt_hbm, held.at[2]), (w_hbm, w_ref)))
    ]
    for load in loads:
        load.start()
    early_chunks = EARLY[level]

    def place(p, lane, slot):
        return rows.at[p, lane * 2 + slot // 4, slot % 4]

    def direct(p):
        copies = [
            remote(
                block.at[p, expert_at(hops)], place(p, 0, slot), x_send.at[p, n], x_recv.at[p, slot], same_core(hops)
            )
            for n, (slot, hops) in enumerate(((1, 1), (3, 3), (2, -2), (4, -1)))
        ]
        return copies + [
            remote(block.at[p, mine], place(p, 1, 0), x_send.at[p, 4], x_recv.at[p, 8], other_core(0))
        ]

    def relay(p, slot):
        return remote(
            place(p, 0, slot), place(p, 0, slot + 4), x_send.at[p, 11 + slot], x_recv.at[p, slot + 4], same_core(-1)
        )

    def forward(p, slot):
        return remote(
            place(p, 0, slot), place(p, 1, slot), x_send.at[p, 4 + slot], x_recv.at[p, 8 + slot], other_core(0)
        )

    def dispatch(p):
        for copy in direct(p):
            copy.start()
        rows[p, 0, 0] = block[p, mine]

    def takes(p, slots):
        for slot in slots:
            remote(
                place(p, 0, slot), place(p, 0, slot), x_send.at[p, 0], x_recv.at[p, slot], other_core(0)
            ).wait_recv()
            if slot < 4:
                relay(p, slot).start()
            forward(p, slot).start()

    def take_lane(p, slots):
        for slot in slots:
            remote(
                place(p, 1, slot), place(p, 1, slot), x_send.at[p, 0], x_recv.at[p, 8 + slot], other_core(0)
            ).wait_recv()

    def place_rows(p, hot, scale):
        value = held[p // CHUNKS, :, columns(p % CHUNKS)]
        if scale is not None:
            value = (scale * value.astype(jnp.float32)).astype(jnp.bfloat16)
        block[p] = dot(hot, value).astype(jnp.bfloat16).reshape(EXPERTS, ROWS, COLS)

    hot = one_hot_of(routes_ref[...]).astype(jnp.bfloat16)
    load_tokens(0).wait()
    place_rows(0, hot, None)
    pl.semaphore_wait(barrier, len(peers))
    dispatch(0)

    def place_x(p):
        load_tokens(p).wait()
        place_rows(p, hot, None)
        dispatch(p)

    over(1, 4, place_x)
    loads[0].wait()
    gates = column(gates_ref[...])
    over(4, 8, lambda p: place_rows(p, hot, gates))
    dispatch(4)
    hot_next = one_hot_of(next_routes_ref[...])
    hot_next_rows = hot_next.astype(jnp.bfloat16)
    loads[1].wait()
    over(8, 12, lambda p: place_rows(p, hot_next_rows, None))
    table[...] = hot_next.T.astype(jnp.bfloat16)
    loads[2].wait()

    def group(kind, q, c):
        return rows[kind * CHUNKS + c, q].reshape(GROUP, COLS)

    def forward_x(q):
        pre_t[q] = jnp.zeros((2 * HID, GROUP), jnp.float32)
        back_t[q] = jnp.zeros((HID, GROUP), jnp.float32)

        def body(c):
            pre_t[q] += dot_last(w_ref[0:2, :, columns(c)].reshape(2 * HID, COLS), group(0, q, c))

        over(0, CHUNKS, body)
        gate = pre_t[q, 0:HID]
        d_t[2, q] = (gate * jax.nn.sigmoid(gate) * pre_t[q, HID:]).astype(jnp.bfloat16)

    def backward(q, c):
        back_t[q] += dot_last(w_ref[2, :, columns(c)], group(1, q, c))

    def slopes(q):
        back = back_t[q]
        gate = pre_t[q, 0:HID]
        up = pre_t[q, HID:]
        logistic = jax.nn.sigmoid(gate)
        d_t[0, q] = (back * up * (logistic * (1.0 + gate * (1.0 - logistic)))).astype(jnp.bfloat16)
        d_t[1, q] = (back * (gate * logistic)).astype(jnp.bfloat16)

    def exchange(index):
        return remote(own.at[index], theirs.at[index], g_send.at[index], g_recv.at[index], partner)

    def exchange_down(c):
        return remote(own_down.at[c], their_down.at[c], f_send.at[c], f_recv.at[c], partner)

    def updated(j, c):
        cols = columns(c)
        grad = jnp.zeros((HID, COLS), jnp.float32)
        for q in range(4):
            grad += dot(d_t[j, q], group(j // 2, q, c))
        grad = grad.astype(jnp.bfloat16).astype(jnp.float32)
        return (w_ref[j, :, cols].astype(jnp.float32) - RATE * grad).astype(jnp.bfloat16)

    def update(j, c, index):
        own[index] = updated(j, c)
        exchange(index).start()

    def update_up(c):
        over(0, 2, lambda j: update(j, c, 2 * c + j))
        takes(8 + c, near)

    def update_down(c):
        value = updated(2, c)
        for n in range(SPLIT):
            own_down[SPLIT * c + n] = value[:, n * FINE : (n + 1) * FINE]
            exchange_down(SPLIT * c + n).start()

    near, rest = (1, 2, 3), (4, 5, 6, 7)
    over(0, 4, lambda p: takes(p, near))
    dispatch(5)

    def forward_half(half):
        @pl.when(half == 1)
        def _():
            over(0, 4, lambda p: takes(p, rest))

        over(0, 4, lambda p: take_lane(p, [4 * half + n for n in range(4)]))
        over(0, 2, lambda lane: forward_x(2 * lane + half))
        takes(4 + half, near)
        dispatch(6 + half)

    over(0, 2, forward_half)

    def early(c):
        takes(c + 4, rest)
        take_lane(c + 4, range(8))

        @pl.when(c < early_chunks)
        def _():
            update_down(c)

        over(0, 4, lambda q: backward(q, c))

        @pl.when(c < 2)
        def _():
            takes(c + 6, near)

    def backward_last(q):
        backward(q, CHUNKS - 1)
        slopes(q)

    over(0, 3, early)
    take_lane(7, (0, 1, 2, 3))
    over(0, 2, lambda lane: backward_last(2 * lane))
    takes(7, rest)
    over(8, 12, dispatch)
    take_lane(7, rest)
    over(0, 2, lambda lane: backward_last(2 * lane + 1))
    over(0, CHUNKS, update_up)
    over(early_chunks, CHUNKS, update_down)

    def averaged(index):
        exchange(index).wait_recv()
        both = own[index].astype(jnp.float32) + theirs[index].astype(jnp.float32)
        return (both * 0.5).astype(jnp.bfloat16)

    def averaged_down(c):
        exchange_down(c).wait_recv()
        both = own_down[c].astype(jnp.float32) + their_down[c].astype(jnp.float32)
        return (both * 0.5).astype(jnp.bfloat16)

    def to_core(c):
        return remote(down.at[0, c], down.at[1, c], d_send.at[0, c], d_recv.at[0, c], other_core(0))

    def to_pair(c):
        return remote(down.at[0, c], down.at[2, c], d_send.at[1, c], d_recv.at[1, c], same_core(-1))

    def pair_to_core(c):
        return remote(down.at[2, c], down.at[3, c], d_send.at[2, c], d_recv.at[2, c], other_core(0))

    def give_back(c, slot):
        return remote(
            out.at[c, slot], ret.at[mine, c], o_send.at[slot - 1, c], o_recv.at[slot - 1, c], same_core(slot)
        )

    def down_start(c):
        down[0, c] = averaged_down(c)
        to_pair(c).start()
        to_core(c).start()

    def down_relay(c):
        to_pair(c).wait_recv()
        pair_to_core(c).start()

    def down_finish(c):
        total = dot(hid[0].reshape(GROUP, HID), down[0, c])
        to_core(c).wait_recv()
        total += dot(hid_in[0].reshape(GROUP, HID), down[1, c])
        total += dot(hid_in[1].reshape(GROUP, HID), down[2, c])
        pair_to_core(c).wait_recv()
        total += dot(hid_in[2].reshape(GROUP, HID), down[3, c])
        out[c] = total.astype(jnp.bfloat16).reshape(4, ROWS, FINE)
        for slot in (3, 2, 1):
            give_back(c, slot).start()
        ret[mine, c] = out[c, 0]

    early_fines = SPLIT * early_chunks
    over(0, early_fines, down_start)
    acc[...] = jnp.zeros_like(acc)

    def average_up(c, j):
        weight = averaged(2 * c + j)
        exchange(2 * c + j).wait_send()
        own[2 * c + j] = weight

    def forward_next(index):
        c, j = index // 2, index % 2

        @pl.when(j == 0)
        def _():
            takes(8 + c, rest)
            take_lane(8 + c, range(8))

        average_up(c, j)

        def body(q):
            acc[j, q] += dot_last(group(2, q, c), own[index])

        over(0, 4, body)

    over(0, 2 * CHUNKS - 1, forward_next)
    average_up(CHUNKS - 1, 1)

    def hidden(n):
        q, to = ((2, other_core(0)), (1, same_core(-1)), (3, other_core(-1)))[n]
        return remote(hid.at[q], hid_in.at[n], h_send.at[n], h_recv.at[n], to)

    def activate(q):
        gate = acc[0, q]
        up = acc[1, q] + dot_last(group(2, q, CHUNKS - 1), own[2 * CHUNKS - 1])
        value = (gate * jax.nn.sigmoid(gate) * up).astype(jnp.bfloat16)
        hid[q] = value.reshape(4, ROWS, HID)

    def activate_send(n):
        activate(3 - n)
        for when, copy in ((0, 2), (1, 0), (2, 1)):

            @pl.when(n == when)
            def _():
                hidden(copy).start()

    over(0, 4, activate_send)
    over(0, early_fines, down_relay)
    down_start(early_fines)
    for n in range(3):
        hidden(n).wait_recv()

    def down_steps(c):
        @pl.when((c >= early_fines - 1) & (c < FINES - 2))
        def _():
            down_start(c + 2)

        @pl.when(c >= early_fines)
        def _():
            down_relay(c)

        down_finish(c)

    over(0, FINES, down_steps)

    next_gates = column(next_gates_ref[...])

    def mix(c, largest):
        for slot, hops in ((1, 1), (2, -2), (3, 3)):
            here = ret.at[expert_at(hops), c]
            remote(here, here, o_send.at[slot - 1, c], o_recv.at[slot - 1, c], other_core(0)).wait_recv()
        value = dot(table[...], ret[:, c].reshape(EXPERTS * ROWS, FINE)) * next_gates
        mixed[c] = value
        return jnp.maximum(largest, jnp.max(jnp.abs(value), axis=1, keepdims=True))

    largest = lax.fori_loop(0, FINES, mix, jnp.zeros((TOK, 1), jnp.float32))
    inverse = 1.0 / (largest + epsilon)

    def code(c):
        codes_ref[:, fine_columns(c)] = (mixed[c] * inverse).astype(jnp.bfloat16)

    over(0, FINES, code)
    lane = lax.broadcasted_iota(jnp.int32, (TOK, TOK), 1)
    across = lax.broadcasted_iota(jnp.int32, (TOK, TOK), 0)
    scales_ref[...] = jnp.sum(jnp.where(lane == across, largest, 0.0), axis=0, keepdims=True)

    def rows_sent(p):
        for copy in direct(p) + [relay(p, slot) for slot in near] + [forward(p, slot) for slot in range(1, 8)]:
            copy.wait_send()

    def chunk_sent(c):
        exchange_down(c).wait_send()
        to_pair(c).wait_send()
        to_core(c).wait_send()
        pair_to_core(c).wait_send()
        for slot in near:
            give_back(c, slot).wait_send()

    over(0, KINDS * CHUNKS, rows_sent)
    for n in range(3):
        hidden(n).wait_send()
    over(0, FINES, chunk_sent)


def step(level, routes, gates, next_routes, next_gates, tokens, cotangent, next_tokens, weights):
    vmem = pl.BlockSpec(memory_space=pltpu.VMEM)
    hbm = pl.BlockSpec(memory_space=pl.ANY)
    bf16, f32 = jnp.bfloat16, jnp.float32
    dma = pltpu.SemaphoreType.DMA
    return pl.pallas_call(
        functools.partial(kernel, level),
        out_shape=(
            jax.ShapeDtypeStruct((TOK, D), bf16),
            jax.ShapeDtypeStruct((1, TOK), f32),
        ),
        in_specs=[vmem] * 4 + [hbm] * 4,
        out_specs=(vmem, vmem),
        scratch_shapes=[
            pltpu.VMEM((3, TOK, D), bf16),
            pltpu.VMEM((3, HID, D), bf16),
            pltpu.VMEM((KINDS * CHUNKS, EXPERTS, ROWS, COLS), bf16),
            pltpu.VMEM((KINDS * CHUNKS, 4, 4, ROWS, COLS), bf16),
            pltpu.VMEM((4, 2 * HID, GROUP), f32),
            pltpu.VMEM((4, HID, GROUP), f32),
            pltpu.VMEM((3, 4, HID, GROUP), bf16),
            pltpu.VMEM((2 * CHUNKS, HID, COLS), bf16),
            pltpu.VMEM((2 * CHUNKS, HID, COLS), bf16),
            pltpu.VMEM((FINES, HID, FINE), bf16),
            pltpu.VMEM((FINES, HID, FINE), bf16),
            pltpu.VMEM((2, 4, GROUP, HID), f32),
            pltpu.VMEM((4, 4, ROWS, HID), bf16),
            pltpu.VMEM((3, 4, ROWS, HID), bf16),
            pltpu.VMEM((4, FINES, HID, FINE), bf16),
            pltpu.VMEM((FINES, 4, ROWS, FINE), bf16),
            pltpu.VMEM((EXPERTS, FINES, ROWS, FINE), bf16),
            pltpu.VMEM((FINES, TOK, FINE), f32),
            pltpu.VMEM((TOK, EXPERTS * ROWS), bf16),
            dma((CHUNKS + 3,)),
            dma((KINDS * CHUNKS, 15)),
            dma((KINDS * CHUNKS, 16)),
            dma((2 * CHUNKS,)),
            dma((2 * CHUNKS,)),
            dma((FINES,)),
            dma((FINES,)),
            dma((3,)),
            dma((3,)),
            dma((3, FINES)),
            dma((3, FINES)),
            dma((3, FINES)),
            dma((3, FINES)),
        ],
        compiler_params=pltpu.CompilerParams(
            collective_id=level, has_side_effects=True, vmem_limit_bytes=48 * 2**20
        ),
        name=f"step_{level}",
    )(routes, gates, next_routes, next_gates, tokens, cotangent, next_tokens, weights)


def local(
    weights,
    tokens,
    cotangent,
    routes,
    gate_weights,
    next_tokens,
    next_routes,
    next_gates,
    step_index,
):
    branches = [functools.partial(step, level) for level in range(LEVELS)]
    codes, scales = lax.switch(
        step_index[0] % LEVELS,
        branches,
        routes.reshape(1, TOK),
        gate_weights.reshape(1, TOK),
        next_routes.reshape(1, TOK),
        next_gates.reshape(1, TOK),
        tokens[0],
        cotangent[0],
        next_tokens[0],
        weights[0],
    )
    return (codes[None], scales)


def solution(mesh):
    placed = (
        P("replica", None, "expert", None),
        P("replica", "expert", None),
        P("replica", "expert", None),
        P("replica", "expert", None),
        P("replica", "expert", None),
        P("replica", "expert", None),
        P("replica", "expert", None),
        P("replica", "expert", None),
        P(),
    )
    return jax.shard_map(
        local,
        mesh=mesh,
        in_specs=placed,
        out_specs=(P("replica", "expert", None), P("replica", "expert")),
        check_vma=False,
    )
```
